32 devices in a mesh: group: 2 (over y), node: 4 (over x, core), tp: 4 (over z).
Axes of the slice: x: 2, y: 2, z: 4, core: 2. Of those that a mesh axis runs over, the one named last changes fastest.
Arguments:
- hidden_in: bfloat16 [64, 3072], P(('group', 'node', 'tp')), parts along dimension 0, may hold values from -6 to 6
- queries: bfloat16 [64, 3072], P(('group', 'node'), 'tp'), parts along dimension 0, may hold values from -8 to 8
- new_keys: bfloat16 [64, 1024], P(('group', 'node'), 'tp'), parts along dimension 0, may hold values from -6 to 6
- new_values: bfloat16 [64, 1024], P(('group', 'node'), 'tp'), parts along dimension 0, may hold values from -6 to 6
- key_cache: bfloat16 [64, 224, 1024], P(('group', 'node'), None, 'tp'), parts along dimension 0, may hold values from -6 to 6
- value_cache: bfloat16 [64, 224, 1024], P(('group', 'node'), None, 'tp'), parts along dimension 0, may hold values from -6 to 6
- lengths: int32 [64], P(('group', 'node')), parts along dimension 0, may hold values from 2 to 224, as said below
- out_weight: bfloat16 [3072, 3072], P('tp'), may hold values from -0.109375 to 0.109375
- norm_gain: float32 [3072], replicated, may hold values from 0.5 to 1.5
- router: bfloat16 [3072, 4], replicated, may hold values from -0.109375 to 0.109375
- expert_ids: int32 [64, 2], P(('group', 'node', 'tp')), parts along dimension 0, may hold values from 0 to 3, all different within a row; in each aligned block of 2 rows (0 to 1, 2 to 3, ...) at most 2 rows name the same one
- gate_weight: bfloat16 [4, 3072, 8192], P('node', None, 'tp'), may hold values from -0.109375 to 0.109375
- up_weight: bfloat16 [4, 3072, 8192], P('node', None, 'tp'), may hold values from -0.109375 to 0.109375
- down_weight: bfloat16 [4, 8192, 3072], P('node', 'tp'), may hold values from -0.0625 to 0.0625
Outputs:
- layer_out: bfloat16 [64, 3072], P(('group', 'node', 'tp')), parts along dimension 0
The draws below stay inside these ranges and needn't reach their ends.
There are 2 independent parts, one for each index of `group`. The reference program is written for one: setup_inputs(seed, part) draws one part's arguments, and reference() takes and returns one part's arrays. A program takes and returns all parts, laid end to end along the dimension named above; an argument that names none is the same for every part. Nothing has to cross between parts.
Inputs may be any that keep to these rules, and one draw needn't show every extreme that they name: `expert_ids`: each row names 2 different experts; in each aligned block of 2 rows (the rows of one device) no expert is named by more than 2 rows. `lengths`: in each aligned block of 2 requests one request uses all 224 cache positions.
All inputs are finite; a program needn't handle non-finite values.
Results may differ from the reference program's by a relative error of at most 0.006.
Values may be sent and summed in bfloat16 or wider, within the bound.
A program may use at most 128 MiB of HBM per device.

```python
import math
import jax
import jax.numpy as jnp
import numpy as np
from jax import lax

D = 3072
HEADS = 24
KV = 8
HD = 128
FF = 8192
EXPERTS = 4
TOP = 2
CTX = 224
ROW_DEV = 2
CAP = 2
SPLIT = 1
REQS = 32


def draw_queries(key, part):
    key = jax.random.fold_in(key, 11)
    result = jnp.clip(jax.random.normal(key, (REQS, HEADS * HD), jnp.float32), -6.0, 6.0)
    return result.astype(jnp.bfloat16)


def draw_key_cache(key, part):
    key = jax.random.fold_in(key, 12)
    result = jnp.clip(jax.random.normal(key, (REQS, CTX, KV * HD), jnp.float32), -6.0, 6.0)
    return result.astype(jnp.bfloat16)


def draw_lengths(key, part):
    key = jax.random.fold_in(key, 13)
    key_base, key_full = jax.random.split(key)
    background = jax.random.randint(key_base, (REQS,), 2, CTX + 1)
    full_choice = jax.random.randint(key_full, (REQS // ROW_DEV,), 0, ROW_DEV)
    full_mask = (jnp.arange(ROW_DEV, dtype=jnp.int32)[None, :] == full_choice[:, None]).reshape(REQS)
    return jnp.where(full_mask, CTX, background).astype(jnp.int32)


def shard_levels(key, shape, cuts, low, largest):
    def one(axis_at, parts):
        heights = jax.random.uniform(jax.random.fold_in(jax.random.fold_in(key, 6), axis_at), (parts,), jnp.float32, low / len(cuts), largest / len(cuts))
        return jnp.repeat(jnp.exp(heights), shape[axis_at] // parts).reshape((-1,) + (1,) * (len(shape) - axis_at - 1))

    factor_of = one(*cuts[0])
    for cut in cuts[1:]:
        factor_of = factor_of * one(*cut)
    return factor_of


def assign_block(stream_key, own, number, rows, count, top, bound, skew):
    ranking = jax.random.permutation(stream_key, count)
    heavy_load, common = load_shares(count, rows * top, bound, skew, True), load_shares(count, rows * top, bound, skew, False)
    places = jnp.arange(count)

    def named(sizes, turn):
        used = int((sizes > 0).sum())
        fixed = max(1, used // 4)
        passed = fixed + (places - fixed + turn * (used - fixed)) % max(1, count - fixed)
        return jnp.zeros((count,), jnp.int32).at[ranking[jnp.where(places < fixed, places, passed)]].set(jnp.asarray(sizes, jnp.int32))

    sizes = jnp.where(number % 4 == 0, named(heavy_load, number // 4), named(common, number - number // 4 - 1))
    mixed = jax.random.permutation(jax.random.fold_in(own, 3), count)
    donor, receiver = mixed[0:count // 2 * 2:2], mixed[1:count // 2 * 2:2]
    room = jnp.minimum(sizes[donor] - 1, bound - sizes[receiver]) // 2
    room = jnp.where((donor == ranking[0]) | (receiver == ranking[0]) | (sizes[receiver] == 0), 0, jnp.maximum(room, 0))
    passed = jax.random.randint(jax.random.fold_in(own, 4), (count // 2,), 0, 1 << 20) % (room + 1)
    sizes = sizes.at[donor].add(-passed).at[receiver].add(passed)
    items = jnp.searchsorted(jnp.cumsum(sizes), jnp.arange(rows * top), side="right").astype(jnp.int32)
    grid = items.reshape(top, rows).T
    grid = grid[jax.random.permutation(jax.random.fold_in(own, 1), rows)]
    turn = jax.random.randint(jax.random.fold_in(own, 2), (rows, 1), 0, top)
    return jnp.take_along_axis(grid, (jnp.arange(top)[None, :] + turn) % top, axis=1)


def load_shares(number_of, total, reach, lean, full):
    loads = [(1 << 20) // math.isqrt(rank ** lean) + 1 for rank in range(1, number_of + 1)]
    largest = reach if full else min(reach, max(-(-total // number_of), total * loads[0] // sum(loads)))
    least = 1 if total - largest >= number_of - 1 else 0
    holding, rest = [largest] + [least] * (number_of - 1), total - largest - least * (number_of - 1)
    while rest > 0:
        candidates = [i for i in range(1, number_of) if holding[i] < largest] or [i for i in range(1, number_of) if holding[i] < reach]
        pool, remaining = sum([loads[i] for i in candidates]), rest
        for i in candidates:
            addition = min(reach - holding[i], max(1, remaining * loads[i] // pool), rest)
            holding[i] = holding[i] + addition
            rest = rest - addition
    return np.array(holding)


def scatter_about(key, extent, width, reach, cuts=(), held_as=jnp.bfloat16):
    drawn = width * jax.random.normal(key, extent, jnp.float32)
    if cuts:
        drawn = drawn * shard_levels(key, extent, cuts, -0.22, 0.18)
    return jnp.clip(drawn, -reach, reach).astype(held_as)


def setup_inputs(seed: int = 0, part: int = 0) -> dict:
    seeds = jax.random.split(jax.random.key(seed), 15)
    part_splits = jax.random.split(jax.random.fold_in(seeds[14], part), 15)
    hidden_in = scatter_about(part_splits[0], (REQS, D), 1.0, 6.0, ((0, 16),))
    queries = draw_queries(jax.random.fold_in(jax.random.fold_in(seeds[14], part), 71), part)
    new_keys = scatter_about(part_splits[2], (REQS, KV * HD), 1.0, 6.0, ((0, 4), (1, 4)))
    new_values = scatter_about(part_splits[3], (REQS, KV * HD), 1.0, 6.0, ((0, 4), (1, 4)))
    key_cache = draw_key_cache(jax.random.fold_in(jax.random.fold_in(seeds[14], part), 71), part)
    value_cache = scatter_about(part_splits[5], (REQS, CTX, KV * HD), 1.0, 6.0, ((0, 4), (2, 4)))
    lengths = draw_lengths(jax.random.fold_in(jax.random.fold_in(seeds[14], part), 71), part)
    out_weight = scatter_about(seeds[7], (HEADS * HD, D), (HEADS * HD) ** -0.5, 0.109375, ((0, 4),))
    norm_gain = jnp.clip(1.0 + 0.1 * jax.random.normal(seeds[8], (D,), jnp.float32), 0.5, 1.5)
    router = scatter_about(seeds[9], (D, EXPERTS), D ** -0.5, 0.109375)
    expert_ids_keys = jax.random.split(jax.random.fold_in(part_splits[10], 1), REQS // ROW_DEV)
    expert_ids_turns = jax.random.permutation(jax.random.fold_in(part_splits[10], 3), REQS // ROW_DEV)
    expert_ids = jax.vmap(lambda own, number: assign_block(jax.random.fold_in(part_splits[10], 2), own, number, ROW_DEV, EXPERTS, TOP, CAP, 2))(expert_ids_keys, expert_ids_turns).reshape((REQS, TOP))
    gate_weight = scatter_about(seeds[11], (EXPERTS * SPLIT, D, FF // SPLIT), D ** -0.5, 0.109375, ((0, 4), (2, 4)))
    up_weight = scatter_about(seeds[12], (EXPERTS * SPLIT, D, FF // SPLIT), D ** -0.5, 0.109375, ((0, 4), (2, 4)))
    down_weight = scatter_about(seeds[13], (EXPERTS * SPLIT, FF // SPLIT, D), FF ** -0.5, 0.0625, ((0, 4), (1, 4)))
    return dict(hidden_in=hidden_in, queries=queries, new_keys=new_keys, new_values=new_values, key_cache=key_cache, value_cache=value_cache, lengths=lengths, out_weight=out_weight, norm_gain=norm_gain, router=router, expert_ids=expert_ids, gate_weight=gate_weight, up_weight=up_weight, down_weight=down_weight)


def attend_block(inputs):
    queries, keys_new, values_new, keys_old, values_old, valid_len = inputs
    request_count = queries.shape[0]
    group_size = HEADS // KV
    scaling = 1.0 / math.sqrt(HD)
    query_heads = queries.astype(jnp.float32).reshape(request_count, KV, group_size, HD)
    key_heads = keys_old.astype(jnp.float32).reshape(request_count, CTX, KV, HD)
    value_heads = values_old.astype(jnp.float32).reshape(request_count, CTX, KV, HD)
    scores = jnp.einsum('rkgd,rckd->rkgc', query_heads, key_heads) * scaling
    own_key = keys_new.astype(jnp.float32).reshape(request_count, KV, HD)
    own_score = jnp.einsum('rkgd,rkd->rkg', query_heads, own_key) * scaling
    positions = jnp.arange(CTX, dtype=jnp.int32)
    usable = positions[None, :] < valid_len[:, None]
    scores = jnp.where(usable[:, None, None, :], scores, -jnp.inf)
    highest = jnp.maximum(lax.optimization_barrier(jnp.max(scores, axis=-1)), own_score)
    weights = jnp.exp(scores - highest[..., None])
    own_weight = jnp.exp(own_score - highest)
    denominator = lax.optimization_barrier(jnp.sum(weights, axis=-1)) + own_weight
    probabilities = lax.optimization_barrier((weights / denominator[..., None]).astype(jnp.bfloat16)).astype(jnp.float32)
    own_prob = lax.optimization_barrier((own_weight / denominator).astype(jnp.bfloat16)).astype(jnp.float32)
    mixture = jnp.einsum('rkgc,rckd->rkgd', probabilities, value_heads)
    own_value = values_new.astype(jnp.float32).reshape(request_count, KV, 1, HD)
    mixture = mixture + own_prob[..., None] * own_value
    return mixture.reshape(request_count, HEADS * HD).astype(jnp.bfloat16)

def reference(hidden_in, queries, new_keys, new_values, key_cache, value_cache, lengths, out_weight, norm_gain, router, expert_ids, gate_weight, up_weight, down_weight):
    blocks = REQS // ROW_DEV

    def shaped(array):
        return array.reshape((blocks, ROW_DEV) + array.shape[1:])
    pieces = tuple((shaped(array) for array in (queries, new_keys, new_values, key_cache, value_cache, lengths)))
    attended = lax.map(attend_block, pieces).reshape(REQS, HEADS * HD)
    projected = jnp.dot(attended, out_weight, preferred_element_type=jnp.float32)
    middle = (hidden_in.astype(jnp.float32) + projected).astype(jnp.bfloat16)
    widened = middle.astype(jnp.float32)
    scale_rms = lax.rsqrt(lax.optimization_barrier(jnp.mean(widened * widened, axis=-1, keepdims=True)) + 1e-05)
    normed = (widened * scale_rms * norm_gain).astype(jnp.bfloat16)
    logits = jnp.dot(normed, router, preferred_element_type=jnp.float32)
    chosen = (expert_ids[:, :, None] == jnp.arange(EXPERTS, dtype=jnp.int32)[None, None, :]).astype(jnp.float32)
    picked = lax.optimization_barrier(jnp.sum(chosen * logits[:, None, :], axis=-1))
    gate_share = jax.nn.sigmoid(picked - picked[:, ::-1])
    mixing = lax.optimization_barrier(jnp.sum(chosen * gate_share[:, :, None], axis=1))
    gate_all = gate_weight.reshape(EXPERTS, SPLIT, D, FF // SPLIT).transpose(0, 2, 1, 3).reshape(EXPERTS, D, FF)
    up_all = up_weight.reshape(EXPERTS, SPLIT, D, FF // SPLIT).transpose(0, 2, 1, 3).reshape(EXPERTS, D, FF)
    down_all = down_weight.reshape(EXPERTS, FF, D)

    def expert_out(weights):
        gate_mat, up_mat, down_mat = weights
        gate_val = jnp.dot(normed, gate_mat, preferred_element_type=jnp.float32)
        up_val = jnp.dot(normed, up_mat, preferred_element_type=jnp.float32)
        hidden_units = (jax.nn.silu(gate_val) * up_val).astype(jnp.bfloat16)
        return jnp.dot(hidden_units, down_mat, preferred_element_type=jnp.float32)
    outputs = lax.map(expert_out, (gate_all, up_all, down_all))
    routed = jnp.einsum('re,erd->rd', mixing, outputs, precision=lax.Precision.HIGHEST)
    return (widened + routed).astype(jnp.bfloat16)
```

```python
import functools
import math

import jax
import jax.numpy as jnp
from jax import lax
from jax.experimental import pallas as pl
from jax.experimental.pallas import tpu as pltpu
from jax.sharding import PartitionSpec as P

HD = 128
LANES = 128
SUB = 8
WIDE = SUB * LANES
MESH = pl.DeviceIdType.MESH
F32 = jnp.float32
BF16 = jnp.bfloat16


def repeat(lo, hi, body):
    if hi - lo <= 16:
        for at in range(lo, hi):
            body(at)
    else:

        def step(at, carry):
            body(at)
            return carry

        lax.fori_loop(lo, hi, step, 0)


def kernel(
    nodes, tps, experts,
    lengths, ids, hidden_in, queries, new_keys, new_values, keys, values,
    out_w, gain, router, gate_w, up_w, down_w,
    out,
    hidden_v, q_v, nk_v, nv_v, k_v, v_v, ow_v, gain_v, router_v, gate_v, up_v, down_v,
    hid_pack, t1, full1, send1, recv1, mid_v, send2, recv2, unpack, lhs, units, lg, t3, send3, recv3,
    local_sem, ow_sem, gate_sem, up_sem, down_sem,
    s1_sem, r1_sem, s2_sem, r2_sem, s3_sem, r3_sem,
):
    count = nodes * tps
    my_node, my_tp = lax.axis_index("node"), lax.axis_index("tp")
    me = my_node * tps + my_tp
    rows = hidden_in.shape[0]
    node_rows = queries.shape[0]
    kv_local = new_keys.shape[1] // HD
    group_size = queries.shape[1] // HD // kv_local
    positions = keys.shape[1]
    wides = hidden_in.shape[1] // WIDE
    unit_chunks, _, unit_wide = gate_v.shape
    split = nodes // experts

    def fetch(src, dst, sem):
        copy = pltpu.make_async_copy(src, dst, sem)
        copy.start()
        return copy

    barrier = pltpu.get_barrier_semaphore()

    def greet(d):
        peer = lax.rem(me + d, count)
        pl.semaphore_signal(
            barrier, inc=1, device_id={"node": peer // tps, "tp": lax.rem(peer, tps)}, device_id_type=MESH
        )

    q_copy = fetch(queries, q_v, local_sem.at[0])
    k_copy = fetch(keys, k_v, local_sem.at[1])
    nk_copy = fetch(new_keys, nk_v, local_sem.at[2])
    v_copy = fetch(values, v_v, local_sem.at[3])
    nv_copy = fetch(new_values, nv_v, local_sem.at[4])
    hidden_copy = fetch(hidden_in, hidden_v, local_sem.at[5])
    gain_copy = fetch(gain, gain_v, local_sem.at[6])
    ow_copies = [
        fetch(out_w.at[:, pl.ds(c * WIDE, WIDE)], ow_v.at[c], ow_sem.at[c]) for c in range(wides)
    ]
    repeat(1, count, greet)
    gate_copies, up_copies = [], []
    for f in range(unit_chunks):
        columns = pl.ds(f * unit_wide, unit_wide)
        gate_copies.append(fetch(gate_w.at[0, :, columns], gate_v.at[f], gate_sem.at[f]))
        up_copies.append(fetch(up_w.at[0, :, columns], up_v.at[f], up_sem.at[f]))
    router_copy = fetch(router, router_v, local_sem.at[7])
    down_copies = [
        fetch(down_w.at[0, :, pl.ds(c * WIDE, WIDE)], down_v.at[c], down_sem.at[c]) for c in range(wides)
    ]

    scaling = 1.0 / math.sqrt(HD)
    row_id = lax.broadcasted_iota(jnp.int32, (node_rows, 1), 0)
    used = jnp.zeros((node_rows, 1), jnp.int32)
    for r in range(node_rows):
        used = jnp.where(row_id == r, lengths[r], used)
    used = jnp.concatenate([used] * group_size, axis=0)
    row_all = jnp.concatenate([row_id] * group_size, axis=0)
    usable = lax.broadcasted_iota(jnp.int32, (group_size * node_rows, positions), 1) < used
    q_copy.wait()
    q_all = q_v[...].astype(F32)
    k_copy.wait()
    nk_copy.wait()
    nk_all = nk_v[...].astype(F32)
    probs, own_probs = [], []
    for k in range(kv_local):
        heads = [
            q_all[:, (k * group_size + g) * HD:(k * group_size + g + 1) * HD] for g in range(group_size)
        ]
        stacked = jnp.concatenate(heads, axis=0)
        stacked16 = stacked.astype(BF16)
        scores = jnp.zeros((group_size * node_rows, positions), F32)
        for r in range(node_rows):
            one = lax.dot_general(
                stacked16, k_v[r, :, k * HD:(k + 1) * HD], (((1,), (1,)), ((), ())), preferred_element_type=F32
            )
            scores = jnp.where(row_all == r, one, scores)
        scores = jnp.where(usable, scores * scaling, -jnp.inf)
        own_key = jnp.concatenate([nk_all[:, k * HD:(k + 1) * HD]] * group_size, axis=0)
        own_score = jnp.sum(stacked * own_key, axis=1, keepdims=True) * scaling
        highest = jnp.maximum(jnp.max(scores, axis=1, keepdims=True), own_score)
        weights = jnp.exp(scores - highest)
        own_weight = jnp.exp(own_score - highest)
        denominator = jnp.sum(weights, axis=1, keepdims=True) + own_weight
        probs.append((weights / denominator).astype(BF16))
        own_probs.append((own_weight / denominator).astype(BF16).astype(F32))
    v_copy.wait()
    nv_copy.wait()
    nv_all = nv_v[...].astype(F32)
    attended = []
    for k in range(kv_local):
        mixture = jnp.zeros((group_size * node_rows, HD), F32)
        for r in range(node_rows):
            one = jnp.dot(probs[k], v_v[r, :, k * HD:(k + 1) * HD], preferred_element_type=F32)
            mixture = jnp.where(row_all == r, one, mixture)
        own_value = jnp.concatenate([nv_all[:, k * HD:(k + 1) * HD]] * group_size, axis=0)
        mixture = mixture + own_probs[k] * own_value
        for g in range(group_size):
            attended.append(mixture[g * node_rows:(g + 1) * node_rows])
    attended = jnp.concatenate(attended, axis=1).astype(BF16)

    hidden_copy.wait()
    hidden_all = hidden_v[...].astype(F32)
    for c in range(wides):
        for i in range(rows):
            for q in range(SUB):
                at = c * WIDE + q * LANES
                hid_pack[c, i * SUB + q:i * SUB + q + 1, :] = hidden_all[i:i + 1, at:at + LANES]

    pl.semaphore_wait(barrier, count - 1)

    def along_tp(d, c):
        peer = lax.rem(my_tp + d, tps)
        return pltpu.make_async_remote_copy(
            src_ref=send1.at[peer, c], dst_ref=recv1.at[my_tp, c],
            send_sem=s1_sem.at[d, c], recv_sem=r1_sem.at[my_tp, c],
            device_id={"tp": peer}, device_id_type=MESH,
        )

    def from_tp(d, c):
        peer = lax.rem(my_tp + d, tps)
        return pltpu.make_async_remote_copy(
            src_ref=send1.at[peer, c], dst_ref=recv1.at[peer, c],
            send_sem=s1_sem.at[d, c], recv_sem=r1_sem.at[peer, c],
            device_id={"tp": peer}, device_id_type=MESH,
        )

    for c in range(wides):
        ow_copies[c].wait()
        partial = jnp.dot(attended, ow_v[c], preferred_element_type=F32)
        for q in range(SUB):
            t1[c, q * node_rows:(q + 1) * node_rows, :] = partial[:, q * LANES:(q + 1) * LANES]
        for j in range(tps):
            block = jnp.concatenate(
                [t1[c, pl.ds(j * rows + i, SUB, stride=node_rows), :] for i in range(rows)], axis=0
            )
            full1[j, c] = block
            send1[j, c] = block.astype(BF16)
        for d in range(1, tps):
            along_tp(d, c).start()

    gain_copy.wait()
    squares = [jnp.zeros((SUB, LANES), F32) for _ in range(rows)]
    for c in range(wides):
        total = full1[my_tp, c]
        for d in range(1, tps):
            from_tp(d, c).wait_recv()
            total = total + recv1[lax.rem(my_tp + d, tps), c].astype(F32)
        middle = (hid_pack[c] + total).astype(BF16).astype(F32)
        mid_v[c] = middle
        for i in range(rows):
            piece = middle[i * SUB:(i + 1) * SUB]
            squares[i] = squares[i] + piece * piece
    scales = []
    for i in range(rows):
        mean = jnp.sum(jnp.sum(squares[i], axis=1, keepdims=True), axis=0, keepdims=True) / (wides * WIDE)
        scales.append(lax.rsqrt(mean + 1e-05))
    for c in range(wides):
        pieces = [mid_v[c, i * SUB:(i + 1) * SUB, :] * scales[i] * gain_v[c] for i in range(rows)]
        normed = jnp.concatenate(pieces, axis=0).astype(BF16)
        send2[c] = normed
        recv2[me, c] = normed

    def spread(d, slot):
        peer = lax.rem(me + d, count)
        return pltpu.make_async_remote_copy(
            src_ref=send2, dst_ref=recv2.at[slot],
            send_sem=s2_sem.at[d], recv_sem=r2_sem.at[slot],
            device_id={"node": peer // tps, "tp": lax.rem(peer, tps)}, device_id_type=MESH,
        )

    repeat(1, count, lambda d: spread(d, me).start())
    repeat(1, count, lambda d: spread(d, lax.rem(me + d, count)).wait_recv())

    for c in range(wides):
        for n in range(nodes):
            for j in range(tps):
                unpack[n, c, j * rows * SUB:(j + 1) * rows * SUB, :] = recv2[n * tps + j, c].astype(F32)
        for q in range(SUB):
            column = jnp.concatenate(
                [unpack[n, c, pl.ds(q, node_rows, stride=SUB), :] for n in range(nodes)], axis=0
            )
            at = c * WIDE + q * LANES
            lhs[:, at:at + LANES] = column.astype(BF16)

    for f in range(unit_chunks):
        gate_copies[f].wait()
        gate = jnp.dot(lhs[...], gate_v[f], preferred_element_type=F32)
        up_copies[f].wait()
        up = jnp.dot(lhs[...], up_v[f], preferred_element_type=F32)
        units[:, f * unit_wide:(f + 1) * unit_wide] = (gate / (1.0 + jnp.exp(-gate)) * up).astype(BF16)

    def give(d, slot, c):
        peer = lax.rem(me + d, count)
        return pltpu.make_async_remote_copy(
            src_ref=send3.at[peer, c], dst_ref=recv3.at[slot, c],
            send_sem=s3_sem.at[d, c], recv_sem=r3_sem.at[slot, c],
            device_id={"node": peer // tps, "tp": lax.rem(peer, tps)}, device_id_type=MESH,
        )

    for c in range(wides):
        down_copies[c].wait()
        share = jnp.dot(units[...], down_v[c], preferred_element_type=F32)
        for n in range(nodes):
            for q in range(SUB):
                t3[c, n, q * node_rows:(q + 1) * node_rows, :] = share[
                    n * node_rows:(n + 1) * node_rows, q * LANES:(q + 1) * LANES
                ]
            for j in range(tps):
                block = jnp.concatenate(
                    [t3[c, n, pl.ds(j * rows + i, SUB, stride=node_rows), :] for i in range(rows)], axis=0
                )
                send3[n * tps + j, c] = block.astype(BF16)
        repeat(1, count, lambda d: give(d, me, c).start())
        recv3[me, c] = send3[me, c]

    router_copy.wait()
    lg[...] = jnp.dot(lhs[...], router_v[...], preferred_element_type=F32)
    mixing = []
    for i in range(rows):
        logit = lg[pl.ds(me * rows + i, 1), :]
        lane = lax.broadcasted_iota(jnp.int32, logit.shape, 1)
        picked = [
            jnp.sum(jnp.where(lane == ids[i, k], logit, 0.0), axis=1, keepdims=True) for k in range(2)
        ]
        gates = [1.0 / (1.0 + jnp.exp(picked[1 - k] - picked[k])) for k in range(2)]
        mixing.append([
            sum(jnp.where(ids[i, k] == e, gates[k], 0.0) for k in range(2)) for e in range(experts)
        ])

    for c in range(wides):
        repeat(1, count, lambda d: give(d, lax.rem(me + d, count), c).wait_recv())
        pieces = []
        sums = [
            functools.reduce(
                lambda a, b: a + b,
                [recv3[s, c].astype(F32) for s in range(e * split * tps, (e + 1) * split * tps)],
            )
            for e in range(experts)
        ]
        for i in range(rows):
            piece = jnp.zeros((SUB, LANES), F32)
            for e in range(experts):
                piece = piece + mixing[i][e] * sums[e][i * SUB:(i + 1) * SUB]
            pieces.append(mid_v[c, i * SUB:(i + 1) * SUB, :] + piece)
        out[c] = jnp.concatenate(pieces, axis=0).astype(BF16)

    for c in range(wides):
        for d in range(1, tps):
            along_tp(d, c).wait_send()
        repeat(1, count, lambda d: give(d, me, c).wait_send())
    repeat(1, count, lambda d: spread(d, me).wait_send())


def local(
    nodes, tps,
    hidden_in, queries, new_keys, new_values, key_cache, value_cache, lengths,
    out_weight, norm_gain, router, expert_ids, gate_weight, up_weight, down_weight,
):
    rows, width = hidden_in.shape
    count = nodes * tps
    node_rows = queries.shape[0]
    wides = width // WIDE
    experts = router.shape[1]
    units = gate_weight.shape[2]
    unit_wide = min(units, 512)
    unit_chunks = units // unit_wide
    total_rows = nodes * node_rows
    depth = out_weight.shape[0]
    packed = (wides, rows * SUB, LANES)
    anywhere = pl.BlockSpec(memory_space=pl.ANY)
    smem = pl.BlockSpec(memory_space=pltpu.SMEM)
    vmem = pltpu.VMEM
    dma = pltpu.SemaphoreType.DMA
    result = pl.pallas_call(
        functools.partial(kernel, nodes, tps, experts),
        out_shape=jax.ShapeDtypeStruct(packed, BF16),
        in_specs=[smem, smem] + [anywhere] * 12,
        out_specs=pl.BlockSpec(memory_space=pltpu.VMEM),
        scratch_shapes=[
            vmem(hidden_in.shape, BF16),
            vmem(queries.shape, BF16),
            vmem(new_keys.shape, BF16),
            vmem(new_values.shape, BF16),
            vmem(key_cache.shape, BF16),
            vmem(value_cache.shape, BF16),
            vmem((wides, depth, WIDE), BF16),
            vmem((wides, SUB, LANES), F32),
            vmem(router.shape, BF16),
            vmem((unit_chunks, width, unit_wide), BF16),
            vmem((unit_chunks, width, unit_wide), BF16),
            vmem((wides, units, WIDE), BF16),
            vmem(packed, F32),
            vmem((wides, SUB * node_rows, LANES), F32),
            vmem((tps,) + packed, F32),
            vmem((tps,) + packed, BF16),
            vmem((tps,) + packed, BF16),
            vmem(packed, F32),
            vmem(packed, BF16),
            vmem((count,) + packed, BF16),
            vmem((nodes, wides, tps * rows * SUB, LANES), F32),
            vmem((total_rows, width), BF16),
            vmem((total_rows, units), BF16),
            vmem((total_rows, experts), F32),
            vmem((wides, nodes, SUB * node_rows, LANES), F32),
            vmem((count,) + packed, BF16),
            vmem((count,) + packed, BF16),
            dma((8,)),
            dma((wides,)),
            dma((unit_chunks,)),
            dma((unit_chunks,)),
            dma((wides,)),
            dma((tps, wides)),
            dma((tps, wides)),
            dma((count,)),
            dma((count,)),
            dma((count, wides)),
            dma((count, wides)),
        ],
        compiler_params=pltpu.CompilerParams(
            collective_id=0, has_side_effects=True, vmem_limit_bytes=60 * 1024 * 1024
        ),
    )(
        lengths, expert_ids, hidden_in, queries, new_keys, new_values, key_cache, value_cache,
        out_weight, norm_gain.reshape(wides, SUB, LANES), router, gate_weight, up_weight, down_weight,
    )
    split_rows = result.reshape(wides, rows, SUB, LANES)
    return jnp.transpose(split_rows, (1, 0, 2, 3)).reshape(rows, width)


def solution(mesh):
    placed = (
        P(("group", "node", "tp"), None),
        P(("group", "node"), "tp"),
        P(("group", "node"), "tp"),
        P(("group", "node"), "tp"),
        P(("group", "node"), None, "tp"),
        P(("group", "node"), None, "tp"),
        P(("group", "node")),
        P("tp", None),
        P(),
        P(),
        P(("group", "node", "tp"), None),
        P("node", None, "tp"),
        P("node", None, "tp"),
        P("node", "tp", None),
    )
    return jax.shard_map(
        functools.partial(local, mesh.shape["node"], mesh.shape["tp"]),
        mesh=mesh,
        in_specs=placed,
        out_specs=P(("group", "node", "tp"), None),
        check_vma=False,
    )
```

```python
import functools
import math

import jax
import jax.numpy as jnp
from jax import lax
from jax.experimental import pallas as pl
from jax.experimental.pallas import tpu as pltpu
from jax.sharding import PartitionSpec as P

HD = 128
LANES = 128
SUB = 8
WIDE = SUB * LANES
MESH = pl.DeviceIdType.MESH
F32 = jnp.float32
BF16 = jnp.bfloat16


def repeat(lo, hi, body):
    if hi - lo <= 16:
        for at in range(lo, hi):
            body(at)
    else:

        def step(at, carry):
            body(at)
            return carry

        lax.fori_loop(lo, hi, step, 0)


def kernel(
    nodes, tps, experts,
    lengths, ids, hidden_in, queries, new_keys, new_values, keys, values,
    out_w, gain, router, gate_w, up_w, down_w,
    out,
    hidden_v, q_v, nk_v, nv_v, k_v, v_v, ow_v, gain_v, router_v, gate_v, up_v, down_v,
    hid_pack, t1, full1, send1, recv1, mid_v, send2, recv2, unpack, lhs, units, lg, t3, send3, recv3, flat,
    local_sem, ow_sem, gate_sem, up_sem, down_sem,
    s1_sem, r1_sem, s2_sem, r2_sem, s3_sem, r3_sem,
):
    count = nodes * tps
    my_node, my_tp = lax.axis_index("node"), lax.axis_index("tp")
    me = my_node * tps + my_tp
    rows = hidden_in.shape[0]
    node_rows = queries.shape[0]
    kv_local = new_keys.shape[1] // HD
    group_size = queries.shape[1] // HD // kv_local
    positions = keys.shape[1]
    wides = hidden_in.shape[1] // WIDE
    unit_chunks, _, unit_wide = gate_v.shape
    split = nodes // experts

    def fetch(src, dst, sem):
        copy = pltpu.make_async_copy(src, dst, sem)
        copy.start()
        return copy

    barrier = pltpu.get_barrier_semaphore()

    def greet(d):
        peer = lax.rem(me + d, count)
        pl.semaphore_signal(
            barrier, inc=1, device_id={"node": peer // tps, "tp": lax.rem(peer, tps)}, device_id_type=MESH
        )

    repeat(1, count, greet)
    q_copy = fetch(queries, q_v, local_sem.at[0])
    k_copy = fetch(keys, k_v, local_sem.at[1])
    nk_copy = fetch(new_keys, nk_v, local_sem.at[2])
    v_copy = fetch(values, v_v, local_sem.at[3])
    nv_copy = fetch(new_values, nv_v, local_sem.at[4])
    hidden_copy = fetch(hidden_in, hidden_v, local_sem.at[5])
    gain_copy = fetch(gain, gain_v, local_sem.at[6])
    ow_copies = [
        fetch(out_w.at[:, pl.ds(c * WIDE, WIDE)], ow_v.at[c], ow_sem.at[c]) for c in range(wides)
    ]
    gate_copies, up_copies, down_copies = [], [], []

    def fetch_units(lo, hi):
        for f in range(lo, hi):
            columns = pl.ds(f * unit_wide, unit_wide)
            gate_copies.append(fetch(gate_w.at[0, :, columns], gate_v.at[f], gate_sem.at[f]))
            up_copies.append(fetch(up_w.at[0, :, columns], up_v.at[f], up_sem.at[f]))


    scaling = 1.0 / math.sqrt(HD)
    row_id = lax.broadcasted_iota(jnp.int32, (node_rows, 1), 0)
    used = jnp.zeros((node_rows, 1), jnp.int32)
    for r in range(node_rows):
        used = jnp.where(row_id == r, lengths[r], used)
    used = jnp.concatenate([used] * group_size, axis=0)
    row_all = jnp.concatenate([row_id] * group_size, axis=0)
    usable = lax.broadcasted_iota(jnp.int32, (group_size * node_rows, positions), 1) < used
    q_copy.wait()
    q_all = q_v[...].astype(F32)
    k_copy.wait()
    fetch_units(0, 1)
    nk_copy.wait()
    nk_all = nk_v[...].astype(F32)
    probs, own_probs = [], []
    for k in range(kv_local):
        heads = [
            q_all[:, (k * group_size + g) * HD:(k * group_size + g + 1) * HD] for g in range(group_size)
        ]
        stacked = jnp.concatenate(heads, axis=0)
        stacked16 = stacked.astype(BF16)
        scores = jnp.zeros((group_size * node_rows, positions), F32)
        for r in range(node_rows):
            one = lax.dot_general(
                stacked16, k_v[r, :, k * HD:(k + 1) * HD], (((1,), (1,)), ((), ())), preferred_element_type=F32
            )
            scores = jnp.where(row_all == r, one, scores)
        scores = jnp.where(usable, scores * scaling, -jnp.inf)
        own_key = jnp.concatenate([nk_all[:, k * HD:(k + 1) * HD]] * group_size, axis=0)
        own_score = jnp.sum(stacked * own_key, axis=1, keepdims=True) * scaling
        highest = jnp.maximum(jnp.max(scores, axis=1, keepdims=True), own_score)
        weights = jnp.exp(scores - highest)
        own_weight = jnp.exp(own_score - highest)
        denominator = jnp.sum(weights, axis=1, keepdims=True) + own_weight
        probs.append((weights / denominator).astype(BF16))
        own_probs.append((own_weight / denominator).astype(BF16).astype(F32))
    v_copy.wait()
    nv_copy.wait()
    fetch_units(1, unit_chunks)
    nv_all = nv_v[...].astype(F32)
    attended = []
    for k in range(kv_local):
        mixture = jnp.zeros((group_size * node_rows, HD), F32)
        for r in range(node_rows):
            one = jnp.dot(probs[k], v_v[r, :, k * HD:(k + 1) * HD], preferred_element_type=F32)
            mixture = jnp.where(row_all == r, one, mixture)
        own_value = jnp.concatenate([nv_all[:, k * HD:(k + 1) * HD]] * group_size, axis=0)
        mixture = mixture + own_probs[k] * own_value
        for g in range(group_size):
            attended.append(mixture[g * node_rows:(g + 1) * node_rows])
    attended = jnp.concatenate(attended, axis=1).astype(BF16)

    hidden_copy.wait()
    hidden_all = hidden_v[...].astype(F32)
    for c in range(wides):
        for i in range(rows):
            for q in range(SUB):
                at = c * WIDE + q * LANES
                hid_pack[c, i * SUB + q:i * SUB + q + 1, :] = hidden_all[i:i + 1, at:at + LANES]

    pl.semaphore_wait(barrier, count - 1)

    def along_tp(d, c):
        peer = lax.rem(my_tp + d, tps)
        return pltpu.make_async_remote_copy(
            src_ref=send1.at[peer, c], dst_ref=recv1.at[my_tp, c],
            send_sem=s1_sem.at[d, c], recv_sem=r1_sem.at[my_tp, c],
            device_id={"tp": peer}, device_id_type=MESH,
        )

    def from_tp(d, c):
        peer = lax.rem(my_tp + d, tps)
        return pltpu.make_async_remote_copy(
            src_ref=send1.at[peer, c], dst_ref=recv1.at[peer, c],
            send_sem=s1_sem.at[d, c], recv_sem=r1_sem.at[peer, c],
            device_id={"tp": peer}, device_id_type=MESH,
        )

    for c in range(wides):
        ow_copies[c].wait()
        partial = jnp.dot(attended, ow_v[c], preferred_element_type=F32)
        for q in range(SUB):
            t1[c, q * node_rows:(q + 1) * node_rows, :] = partial[:, q * LANES:(q + 1) * LANES]
        for j in range(tps):
            block = jnp.concatenate(
                [t1[c, pl.ds(j * rows + i, SUB, stride=node_rows), :] for i in range(rows)], axis=0
            )
            full1[j, c] = block
            send1[j, c] = block.astype(BF16)
        for d in range(1, tps):
            along_tp(d, c).start()

    router_copy = fetch(router, router_v, local_sem.at[7])
    for c in range(wides):
        down_copies.append(
            fetch(down_w.at[0, :, pl.ds(c * WIDE, WIDE)], down_v.at[c], down_sem.at[c])
        )
    gain_copy.wait()
    squares = [jnp.zeros((SUB, LANES), F32) for _ in range(rows)]
    for c in range(wides):
        total = full1[my_tp, c]
        for d in range(1, tps):
            from_tp(d, c).wait_recv()
            total = total + recv1[lax.rem(my_tp + d, tps), c].astype(F32)
        middle = (hid_pack[c] + total).astype(BF16).astype(F32)
        mid_v[c] = middle
        for i in range(rows):
            piece = middle[i * SUB:(i + 1) * SUB]
            squares[i] = squares[i] + piece * piece
    scales = []
    for i in range(rows):
        mean = jnp.sum(jnp.sum(squares[i], axis=1, keepdims=True), axis=0, keepdims=True) / (wides * WIDE)
        scales.append(lax.rsqrt(mean + 1e-05))
    for c in range(wides):
        pieces = [mid_v[c, i * SUB:(i + 1) * SUB, :] * scales[i] * gain_v[c] for i in range(rows)]
        normed = jnp.concatenate(pieces, axis=0).astype(BF16)
        send2[c] = normed
        recv2[me, c] = normed

    def spread(d, slot):
        peer = lax.rem(me + d, count)
        return pltpu.make_async_remote_copy(
            src_ref=send2, dst_ref=recv2.at[slot],
            send_sem=s2_sem.at[d], recv_sem=r2_sem.at[slot],
            device_id={"node": peer // tps, "tp": lax.rem(peer, tps)}, device_id_type=MESH,
        )

    repeat(1, count, lambda d: spread(d, me).start())
    repeat(1, count, lambda d: spread(d, lax.rem(me + d, count)).wait_recv())

    for c in range(wides):
        for n in range(nodes):
            for j in range(tps):
                unpack[n, c, j * rows * SUB:(j + 1) * rows * SUB, :] = recv2[n * tps + j, c].astype(F32)
        for q in range(SUB):
            column = jnp.concatenate(
                [unpack[n, c, pl.ds(q, node_rows, stride=SUB), :] for n in range(nodes)], axis=0
            )
            at = c * WIDE + q * LANES
            lhs[:, at:at + LANES] = column.astype(BF16)

    for f in range(unit_chunks):
        gate_copies[f].wait()
        gate = jnp.dot(lhs[...], gate_v[f], preferred_element_type=F32)
        up_copies[f].wait()
        up = jnp.dot(lhs[...], up_v[f], preferred_element_type=F32)
        units[:, f * unit_wide:(f + 1) * unit_wide] = (gate / (1.0 + jnp.exp(-gate)) * up).astype(BF16)

    def give(d, slot, c):
        peer = lax.rem(me + d, count)
        return pltpu.make_async_remote_copy(
            src_ref=send3.at[peer, c], dst_ref=recv3.at[slot, c],
            send_sem=s3_sem.at[d, c], recv_sem=r3_sem.at[slot, c],
            device_id={"node": peer // tps, "tp": lax.rem(peer, tps)}, device_id_type=MESH,
        )

    for c in range(wides):
        down_copies[c].wait()
        share = jnp.dot(units[...], down_v[c], preferred_element_type=F32)
        for n in range(nodes):
            for q in range(SUB):
                t3[c, n, q * node_rows:(q + 1) * node_rows, :] = share[
                    n * node_rows:(n + 1) * node_rows, q * LANES:(q + 1) * LANES
                ]
            for j in range(tps):
                block = jnp.concatenate(
                    [t3[c, n, pl.ds(j * rows + i, SUB, stride=node_rows), :] for i in range(rows)], axis=0
                )
                send3[n * tps + j, c] = block.astype(BF16)
        repeat(1, count, lambda d: give(d, me, c).start())
        recv3[me, c] = send3[me, c]

    router_copy.wait()
    lg[...] = lax.dot_general(
        lhs[...], router_v[...], (((1,), (1,)), ((), ())), preferred_element_type=F32
    )
    mixing = []
    for i in range(rows):
        logit = lg[pl.ds(me * rows + i, 1), :]
        lane = lax.broadcasted_iota(jnp.int32, logit.shape, 1)
        picked = [
            jnp.sum(jnp.where(lane == ids[i, k], logit, 0.0), axis=1, keepdims=True) for k in range(2)
        ]
        gates = [1.0 / (1.0 + jnp.exp(picked[1 - k] - picked[k])) for k in range(2)]
        mixing.append([
            sum(jnp.where(ids[i, k] == e, gates[k], 0.0) for k in range(2)) for e in range(experts)
        ])

    for c in range(wides):
        repeat(1, count, lambda d: give(d, lax.rem(me + d, count), c).wait_recv())
        sums = [
            functools.reduce(
                lambda a, b: a + b,
                [recv3[s, c].astype(F32) for s in range(e * split * tps, (e + 1) * split * tps)],
            )
            for e in range(experts)
        ]
        for i in range(rows):
            piece = jnp.zeros((SUB, LANES), F32)
            for e in range(experts):
                piece = piece + mixing[i][e] * sums[e][i * SUB:(i + 1) * SUB]
            piece = mid_v[c, i * SUB:(i + 1) * SUB, :] + piece
            for q in range(SUB):
                at = c * WIDE + q * LANES
                flat[i:i + 1, at:at + LANES] = piece[q:q + 1]
    out[...] = flat[...].astype(BF16)

    for c in range(wides):
        for d in range(1, tps):
            along_tp(d, c).wait_send()
        repeat(1, count, lambda d: give(d, me, c).wait_send())
    repeat(1, count, lambda d: spread(d, me).wait_send())


def local(
    nodes, tps,
    hidden_in, queries, new_keys, new_values, key_cache, value_cache, lengths,
    out_weight, norm_gain, router, expert_ids, gate_weight, up_weight, down_weight,
):
    rows, width = hidden_in.shape
    count = nodes * tps
    node_rows = queries.shape[0]
    wides = width // WIDE
    experts = router.shape[1]
    units = gate_weight.shape[2]
    unit_wide = min(units, 512)
    unit_chunks = units // unit_wide
    total_rows = nodes * node_rows
    depth = out_weight.shape[0]
    packed = (wides, rows * SUB, LANES)
    anywhere = pl.BlockSpec(memory_space=pl.ANY)
    smem = pl.BlockSpec(memory_space=pltpu.SMEM)
    vmem = pltpu.VMEM
    dma = pltpu.SemaphoreType.DMA
    return pl.pallas_call(
        functools.partial(kernel, nodes, tps, experts),
        out_shape=jax.ShapeDtypeStruct((rows, width), BF16),
        in_specs=[smem, smem] + [anywhere] * 12,
        out_specs=pl.BlockSpec(memory_space=pltpu.VMEM),
        scratch_shapes=[
            vmem(hidden_in.shape, BF16),
            vmem(queries.shape, BF16),
            vmem(new_keys.shape, BF16),
            vmem(new_values.shape, BF16),
            vmem(key_cache.shape, BF16),
            vmem(value_cache.shape, BF16),
            vmem((wides, depth, WIDE), BF16),
            vmem((wides, SUB, LANES), F32),
            vmem(router.shape[::-1], BF16),
            vmem((unit_chunks, width, unit_wide), BF16),
            vmem((unit_chunks, width, unit_wide), BF16),
            vmem((wides, units, WIDE), BF16),
            vmem(packed, F32),
            vmem((wides, SUB * node_rows, LANES), F32),
            vmem((tps,) + packed, F32),
            vmem((tps,) + packed, BF16),
            vmem((tps,) + packed, BF16),
            vmem(packed, F32),
            vmem(packed, BF16),
            vmem((count,) + packed, BF16),
            vmem((nodes, wides, tps * rows * SUB, LANES), F32),
            vmem((total_rows, width), BF16),
            vmem((total_rows, units), BF16),
            vmem((total_rows, experts), F32),
            vmem((wides, nodes, SUB * node_rows, LANES), F32),
            vmem((count,) + packed, BF16),
            vmem((count,) + packed, BF16),
            vmem((rows, width), F32),
            dma((8,)),
            dma((wides,)),
            dma((unit_chunks,)),
            dma((unit_chunks,)),
            dma((wides,)),
            dma((tps, wides)),
            dma((tps, wides)),
            dma((count,)),
            dma((count,)),
            dma((count, wides)),
            dma((count, wides)),
        ],
        compiler_params=pltpu.CompilerParams(
            collective_id=0, has_side_effects=True, vmem_limit_bytes=60 * 1024 * 1024
        ),
    )(
        lengths, expert_ids, hidden_in, queries, new_keys, new_values, key_cache, value_cache,
        out_weight, norm_gain.reshape(wides, SUB, LANES), router.T, gate_weight, up_weight, down_weight,
    )


def solution(mesh):
    placed = (
        P(("group", "node", "tp"), None),
        P(("group", "node"), "tp"),
        P(("group", "node"), "tp"),
        P(("group", "node"), "tp"),
        P(("group", "node"), None, "tp"),
        P(("group", "node"), None, "tp"),
        P(("group", "node")),
        P("tp", None),
        P(),
        P(),
        P(("group", "node", "tp"), None),
        P("node", None, "tp"),
        P("node", None, "tp"),
        P("node", "tp", None),
    )
    return jax.shard_map(
        functools.partial(local, mesh.shape["node"], mesh.shape["tp"]),
        mesh=mesh,
        in_specs=placed,
        out_specs=P(("group", "node", "tp"), None),
        check_vma=False,
    )
```

```python
import functools
import math

import jax
import jax.numpy as jnp
from jax import lax
from jax.experimental import pallas as pl
from jax.experimental.pallas import tpu as pltpu
from jax.sharding import PartitionSpec as P

HD = 128
LANES = 128
SUB = 8
WIDE = SUB * LANES
MESH = pl.DeviceIdType.MESH
F32 = jnp.float32
BF16 = jnp.bfloat16


def repeat(lo, hi, body):
    if hi - lo <= 16:
        for at in range(lo, hi):
            body(at)
    else:

        def step(at, carry):
            body(at)
            return carry

        lax.fori_loop(lo, hi, step, 0)


def kernel(
    nodes, tps, experts,
    lengths, ids, hidden_in, queries, new_keys, new_values, keys, values,
    out_w, gain, router, gate_w, up_w, down_w,
    out,
    hidden_v, q_v, nk_v, nv_v, k_v, v_v, ow_v, gain_v, router_v, gate_v, up_v, down_v,
    hid_pack, t1, full1, send1, recv1, mid_v, send2, recv2, unpack, lhs, units, lg, t3, send3, recv3, flat,
    local_sem, ow_sem, gate_sem, up_sem, down_sem,
    s1_sem, r1_sem, s2_sem, r2_sem, s3_sem, r3_sem,
):
    count = nodes * tps
    my_node, my_tp = lax.axis_index("node"), lax.axis_index("tp")
    me = my_node * tps + my_tp
    rows = hidden_in.shape[0]
    node_rows = queries.shape[0]
    kv_local = new_keys.shape[1] // HD
    group_size = queries.shape[1] // HD // kv_local
    positions = keys.shape[1]
    wides = hidden_in.shape[1] // WIDE
    unit_chunks, _, unit_wide = gate_v.shape
    split = nodes // experts

    def fetch(src, dst, sem):
        copy = pltpu.make_async_copy(src, dst, sem)
        copy.start()
        return copy

    barrier = pltpu.get_barrier_semaphore()

    def greet(d):
        peer = lax.rem(me + d, count)
        pl.semaphore_signal(
            barrier, inc=1, device_id={"node": peer // tps, "tp": lax.rem(peer, tps)}, device_id_type=MESH
        )

    repeat(1, count, greet)
    q_copy = fetch(queries, q_v, local_sem.at[0])
    k_copy = fetch(keys, k_v, local_sem.at[1])
    nk_copy = fetch(new_keys, nk_v, local_sem.at[2])
    v_copy = fetch(values, v_v, local_sem.at[3])
    nv_copy = fetch(new_values, nv_v, local_sem.at[4])
    hidden_copy = fetch(hidden_in, hidden_v, local_sem.at[5])
    gain_copy = fetch(gain, gain_v, local_sem.at[6])
    ow_copies = [
        fetch(out_w.at[:, pl.ds(c * WIDE, WIDE)], ow_v.at[c], ow_sem.at[c]) for c in range(wides)
    ]
    gate_copies, up_copies, down_copies = [], [], []

    def fetch_units(lo, hi):
        for f in range(lo, hi):
            columns = pl.ds(f * unit_wide, unit_wide)
            gate_copies.append(fetch(gate_w.at[0, :, columns], gate_v.at[f], gate_sem.at[f]))
            up_copies.append(fetch(up_w.at[0, :, columns], up_v.at[f], up_sem.at[f]))


    scaling = 1.0 / math.sqrt(HD)
    row_id = lax.broadcasted_iota(jnp.int32, (node_rows, 1), 0)
    used = jnp.zeros((node_rows, 1), jnp.int32)
    for r in range(node_rows):
        used = jnp.where(row_id == r, lengths[r], used)
    used = jnp.concatenate([used] * group_size, axis=0)
    row_all = jnp.concatenate([row_id] * group_size, axis=0)
    usable = lax.broadcasted_iota(jnp.int32, (group_size * node_rows, positions), 1) < used
    q_copy.wait()
    q_all = q_v[...].astype(F32)
    k_copy.wait()
    fetch_units(0, 1)
    nk_copy.wait()
    nk_all = nk_v[...].astype(F32)
    probs, own_probs = [], []
    for k in range(kv_local):
        heads = [
            q_all[:, (k * group_size + g) * HD:(k * group_size + g + 1) * HD] for g in range(group_size)
        ]
        stacked = jnp.concatenate(heads, axis=0)
        stacked16 = stacked.astype(BF16)
        scores = jnp.zeros((group_size * node_rows, positions), F32)
        for r in range(node_rows):
            one = lax.dot_general(
                stacked16, k_v[r, :, k * HD:(k + 1) * HD], (((1,), (1,)), ((), ())), preferred_element_type=F32
            )
            scores = jnp.where(row_all == r, one, scores)
        scores = jnp.where(usable, scores * scaling, -jnp.inf)
        own_key = jnp.concatenate([nk_all[:, k * HD:(k + 1) * HD]] * group_size, axis=0)
        own_score = jnp.sum(stacked * own_key, axis=1, keepdims=True) * scaling
        highest = jnp.maximum(jnp.max(scores, axis=1, keepdims=True), own_score)
        weights = jnp.exp(scores - highest)
        own_weight = jnp.exp(own_score - highest)
        denominator = jnp.sum(weights, axis=1, keepdims=True) + own_weight
        probs.append((weights / denominator).astype(BF16))
        own_probs.append((own_weight / denominator).astype(BF16).astype(F32))
    v_copy.wait()
    nv_copy.wait()
    fetch_units(1, unit_chunks)
    nv_all = nv_v[...].astype(F32)
    attended = []
    for k in range(kv_local):
        mixture = jnp.zeros((group_size * node_rows, HD), F32)
        for r in range(node_rows):
            one = jnp.dot(probs[k], v_v[r, :, k * HD:(k + 1) * HD], preferred_element_type=F32)
            mixture = jnp.where(row_all == r, one, mixture)
        own_value = jnp.concatenate([nv_all[:, k * HD:(k + 1) * HD]] * group_size, axis=0)
        mixture = mixture + own_probs[k] * own_value
        for g in range(group_size):
            attended.append(mixture[g * node_rows:(g + 1) * node_rows])
    attended = jnp.concatenate(attended, axis=1).astype(BF16)

    hidden_copy.wait()
    hidden_all = hidden_v[...].astype(F32)
    for c in range(wides):
        for i in range(rows):
            for q in range(SUB):
                at = c * WIDE + q * LANES
                hid_pack[c, i * SUB + q:i * SUB + q + 1, :] = hidden_all[i:i + 1, at:at + LANES]

    pl.semaphore_wait(barrier, count - 1)

    def along_tp(d, c):
        peer = lax.rem(my_tp + d, tps)
        return pltpu.make_async_remote_copy(
            src_ref=send1.at[peer, c], dst_ref=recv1.at[my_tp, c],
            send_sem=s1_sem.at[d, c], recv_sem=r1_sem.at[my_tp, c],
            device_id={"tp": peer}, device_id_type=MESH,
        )

    def from_tp(d, c):
        peer = lax.rem(my_tp + d, tps)
        return pltpu.make_async_remote_copy(
            src_ref=send1.at[peer, c], dst_ref=recv1.at[peer, c],
            send_sem=s1_sem.at[d, c], recv_sem=r1_sem.at[peer, c],
            device_id={"tp": peer}, device_id_type=MESH,
        )

    for c in range(wides):
        ow_copies[c].wait()
        partial = jnp.dot(attended, ow_v[c], preferred_element_type=F32)
        for q in range(SUB):
            t1[c, q * node_rows:(q + 1) * node_rows, :] = partial[:, q * LANES:(q + 1) * LANES]
        for j in range(tps):
            block = jnp.concatenate(
                [t1[c, pl.ds(j * rows + i, SUB, stride=node_rows), :] for i in range(rows)], axis=0
            )
            full1[j, c] = block
            send1[j, c] = block.astype(BF16)
        for d in range(1, tps):
            along_tp(d, c).start()

    router_copy = fetch(router, router_v, local_sem.at[7])
    for c in range(wides):
        down_copies.append(
            fetch(down_w.at[0, :, pl.ds(c * WIDE, WIDE)], down_v.at[c], down_sem.at[c])
        )
    gain_copy.wait()
    squares = [jnp.zeros((SUB, LANES), F32) for _ in range(rows)]
    for c in range(wides):
        total = full1[my_tp, c]
        for d in range(1, tps):
            from_tp(d, c).wait_recv()
            total = total + recv1[lax.rem(my_tp + d, tps), c].astype(F32)
        middle = (hid_pack[c] + total).astype(BF16).astype(F32)
        mid_v[c] = middle
        for i in range(rows):
            piece = middle[i * SUB:(i + 1) * SUB]
            squares[i] = squares[i] + piece * piece
    scales = []
    for i in range(rows):
        mean = jnp.sum(jnp.sum(squares[i], axis=1, keepdims=True), axis=0, keepdims=True) / (wides * WIDE)
        scales.append(lax.rsqrt(mean + 1e-05))
    for c in range(wides):
        pieces = [mid_v[c, i * SUB:(i + 1) * SUB, :] * scales[i] * gain_v[c] for i in range(rows)]
        normed = jnp.concatenate(pieces, axis=0).astype(BF16)
        send2[c] = normed
        recv2[me, c] = normed

    pairs = count // 2
    core = lax.rem(my_node, 2)
    partner = {"node": my_node + 1 - 2 * core, "tp": my_tp}
    my_pair = my_node // 2 * tps + my_tp

    def device_of(pair, of_core):
        return pair // tps * 2 + of_core, lax.rem(pair, tps)

    def slot_of(pair, of_core):
        node, at = device_of(pair, of_core)
        return node * tps + at

    def spread(d):
        node, at = device_of(lax.rem(my_pair + d, pairs), core)
        return pltpu.make_async_remote_copy(
            src_ref=send2, dst_ref=recv2.at[me], send_sem=s2_sem.at[d], recv_sem=r2_sem.at[me],
            device_id={"node": node, "tp": at}, device_id_type=MESH,
        )

    def hand(d, of_core):
        slot = slot_of(lax.rem(my_pair + pairs - d, pairs), of_core)
        return pltpu.make_async_remote_copy(
            src_ref=recv2.at[slot], dst_ref=recv2.at[slot],
            send_sem=s2_sem.at[pairs + d], recv_sem=r2_sem.at[slot],
            device_id=partner, device_id_type=MESH,
        )

    def pass_on(d):
        hand(d, core).wait_recv()
        hand(d, core).start()

    repeat(1, pairs, lambda d: spread(d).start())
    hand(0, core).start()
    repeat(1, pairs, pass_on)
    repeat(0, pairs, lambda d: hand(d, 1 - core).wait_recv())

    for c in range(wides):
        for n in range(nodes):
            for j in range(tps):
                unpack[n, c, j * rows * SUB:(j + 1) * rows * SUB, :] = recv2[n * tps + j, c].astype(F32)
        for q in range(SUB):
            column = jnp.concatenate(
                [unpack[n, c, pl.ds(q, node_rows, stride=SUB), :] for n in range(nodes)], axis=0
            )
            at = c * WIDE + q * LANES
            lhs[:, at:at + LANES] = column.astype(BF16)

    for f in range(unit_chunks):
        gate_copies[f].wait()
        gate = jnp.dot(lhs[...], gate_v[f], preferred_element_type=F32)
        up_copies[f].wait()
        up = jnp.dot(lhs[...], up_v[f], preferred_element_type=F32)
        units[:, f * unit_wide:(f + 1) * unit_wide] = (gate / (1.0 + jnp.exp(-gate)) * up).astype(BF16)

    def give(d, slot, c):
        peer = lax.rem(me + d, count)
        return pltpu.make_async_remote_copy(
            src_ref=send3.at[peer, c], dst_ref=recv3.at[slot, c],
            send_sem=s3_sem.at[d, c], recv_sem=r3_sem.at[slot, c],
            device_id={"node": peer // tps, "tp": lax.rem(peer, tps)}, device_id_type=MESH,
        )

    for c in range(wides):
        down_copies[c].wait()
        share = jnp.dot(units[...], down_v[c], preferred_element_type=F32)
        for n in range(nodes):
            for q in range(SUB):
                t3[c, n, q * node_rows:(q + 1) * node_rows, :] = share[
                    n * node_rows:(n + 1) * node_rows, q * LANES:(q + 1) * LANES
                ]
            for j in range(tps):
                block = jnp.concatenate(
                    [t3[c, n, pl.ds(j * rows + i, SUB, stride=node_rows), :] for i in range(rows)], axis=0
                )
                send3[n * tps + j, c] = block.astype(BF16)
        repeat(1, count, lambda d: give(d, me, c).start())
        recv3[me, c] = send3[me, c]

    router_copy.wait()
    lg[...] = lax.dot_general(
        lhs[...], router_v[...], (((1,), (1,)), ((), ())), preferred_element_type=F32
    )
    mixing = []
    for i in range(rows):
        logit = lg[pl.ds(me * rows + i, 1), :]
        lane = lax.broadcasted_iota(jnp.int32, logit.shape, 1)
        picked = [
            jnp.sum(jnp.where(lane == ids[i, k], logit, 0.0), axis=1, keepdims=True) for k in range(2)
        ]
        gates = [1.0 / (1.0 + jnp.exp(picked[1 - k] - picked[k])) for k in range(2)]
        mixing.append([
            sum(jnp.where(ids[i, k] == e, gates[k], 0.0) for k in range(2)) for e in range(experts)
        ])

    for c in range(wides):
        repeat(1, count, lambda d: give(d, lax.rem(me + d, count), c).wait_recv())
        sums = [
            functools.reduce(
                lambda a, b: a + b,
                [recv3[s, c].astype(F32) for s in range(e * split * tps, (e + 1) * split * tps)],
            )
            for e in range(experts)
        ]
        for i in range(rows):
            piece = jnp.zeros((SUB, LANES), F32)
            for e in range(experts):
                piece = piece + mixing[i][e] * sums[e][i * SUB:(i + 1) * SUB]
            piece = mid_v[c, i * SUB:(i + 1) * SUB, :] + piece
            for q in range(SUB):
                at = c * WIDE + q * LANES
                flat[i:i + 1, at:at + LANES] = piece[q:q + 1]
    out[...] = flat[...].astype(BF16)

    for c in range(wides):
        for d in range(1, tps):
            along_tp(d, c).wait_send()
        repeat(1, count, lambda d: give(d, me, c).wait_send())
    repeat(1, pairs, lambda d: spread(d).wait_send())
    repeat(0, pairs, lambda d: hand(d, core).wait_send())


def local(
    nodes, tps,
    hidden_in, queries, new_keys, new_values, key_cache, value_cache, lengths,
    out_weight, norm_gain, router, expert_ids, gate_weight, up_weight, down_weight,
):
    rows, width = hidden_in.shape
    count = nodes * tps
    node_rows = queries.shape[0]
    wides = width // WIDE
    experts = router.shape[1]
    units = gate_weight.shape[2]
    unit_wide = min(units, 512)
    unit_chunks = units // unit_wide
    total_rows = nodes * node_rows
    depth = out_weight.shape[0]
    packed = (wides, rows * SUB, LANES)
    anywhere = pl.BlockSpec(memory_space=pl.ANY)
    smem = pl.BlockSpec(memory_space=pltpu.SMEM)
    vmem = pltpu.VMEM
    dma = pltpu.SemaphoreType.DMA
    return pl.pallas_call(
        functools.partial(kernel, nodes, tps, experts),
        out_shape=jax.ShapeDtypeStruct((rows, width), BF16),
        in_specs=[smem, smem] + [anywhere] * 12,
        out_specs=pl.BlockSpec(memory_space=pltpu.VMEM),
        scratch_shapes=[
            vmem(hidden_in.shape, BF16),
            vmem(queries.shape, BF16),
            vmem(new_keys.shape, BF16),
            vmem(new_values.shape, BF16),
            vmem(key_cache.shape, BF16),
            vmem(value_cache.shape, BF16),
            vmem((wides, depth, WIDE), BF16),
            vmem((wides, SUB, LANES), F32),
            vmem(router.shape[::-1], BF16),
            vmem((unit_chunks, width, unit_wide), BF16),
            vmem((unit_chunks, width, unit_wide), BF16),
            vmem((wides, units, WIDE), BF16),
            vmem(packed, F32),
            vmem((wides, SUB * node_rows, LANES), F32),
            vmem((tps,) + packed, F32),
            vmem((tps,) + packed, BF16),
            vmem((tps,) + packed, BF16),
            vmem(packed, F32),
            vmem(packed, BF16),
            vmem((count,) + packed, BF16),
            vmem((nodes, wides, tps * rows * SUB, LANES), F32),
            vmem((total_rows, width), BF16),
            vmem((total_rows, units), BF16),
            vmem((total_rows, experts), F32),
            vmem((wides, nodes, SUB * node_rows, LANES), F32),
            vmem((count,) + packed, BF16),
            vmem((count,) + packed, BF16),
            vmem((rows, width), F32),
            dma((8,)),
            dma((wides,)),
            dma((unit_chunks,)),
            dma((unit_chunks,)),
            dma((wides,)),
            dma((tps, wides)),
            dma((tps, wides)),
            dma((count,)),
            dma((count,)),
            dma((count, wides)),
            dma((count, wides)),
        ],
        compiler_params=pltpu.CompilerParams(
            collective_id=0, has_side_effects=True, vmem_limit_bytes=60 * 1024 * 1024
        ),
    )(
        lengths, expert_ids, hidden_in, queries, new_keys, new_values, key_cache, value_cache,
        out_weight, norm_gain.reshape(wides, SUB, LANES), router.T, gate_weight, up_weight, down_weight,
    )


def solution(mesh):
    placed = (
        P(("group", "node", "tp"), None),
        P(("group", "node"), "tp"),
        P(("group", "node"), "tp"),
        P(("group", "node"), "tp"),
        P(("group", "node"), None, "tp"),
        P(("group", "node"), None, "tp"),
        P(("group", "node")),
        P("tp", None),
        P(),
        P(),
        P(("group", "node", "tp"), None),
        P("node", None, "tp"),
        P("node", None, "tp"),
        P("node", "tp", None),
    )
    return jax.shard_map(
        functools.partial(local, mesh.shape["node"], mesh.shape["tp"]),
        mesh=mesh,
        in_specs=placed,
        out_specs=P(("group", "node", "tp"), None),
        check_vma=False,
    )
```
